512 devices in a mesh: gossip: 64 (over z, y_hi, core), tensor: 8 (over x, y_lo).
Axes of the slice: x: 4, y: 4 (y_hi: 2, y_lo: 2; y = y_hi * 2 + y_lo), z: 16, core: 2. Of those that a mesh axis runs over, the one named last changes fastest.
Arguments:
- inputs: bfloat16 [2, 2048, 20480], P(None, 'tensor', 'gossip'), may hold values from -6 to 6
- cotangent: bfloat16 [2, 2048, 20480], P(None, 'tensor', 'gossip'), may hold values from -6 to 6
- numerators: bfloat16 [64, 2048, 2048], P('gossip', None, 'tensor'), may hold values from -6 to 6
- momentum: bfloat16 [64, 2048, 2048], P('gossip', None, 'tensor'), may hold values from -6 to 6
- push_weight: float32 [64], P('gossip'), may hold values from 0.5 to 2
- step_index: int32 [], replicated, may hold values from 0 to 999
Outputs:
- numerators_out: bfloat16 [64, 2048, 2048], P('gossip', None, 'tensor')
- momentum_out: bfloat16 [64, 2048, 2048], P('gossip', None, 'tensor')
- weight_out: float32 [64], P('gossip')
- input_grads: bfloat16 [2, 2048, 20480], P(None, 'tensor', 'gossip')
The draws below stay inside these ranges and needn't reach their ends.
All inputs are finite; a program needn't handle non-finite values.
Results may differ from the reference program's by a relative error of at most 0.02.
Values may be sent and summed in bfloat16 or wider, within the bound.
No kernel may reach another device: no remote copies, remote signals or barrier semaphores. Data moves between devices by JAX's collectives and lax.ppermute only.
A program may use at most 64 MiB of HBM per device.

```python
import math
import jax
import jax.numpy as jnp
from jax import lax

DIN = 2048
HEAD_DIM = 128
TOK = 320
STEPS = 2
DOUT = 2048
REPLICAS = 64
TOKENS = 20480
N_GOSSIP = 64
N_TENSOR = 8


def shard_levels(rng, extent, cuts, least, high):
    factor_of = 1.0
    for axis_at, shards_of in cuts:
        draws = jax.random.uniform(jax.random.fold_in(jax.random.fold_in(rng, 6), axis_at), (shards_of,), jnp.float32, least / len(cuts), high / len(cuts))
        factor_of = factor_of * jnp.repeat(jnp.exp(draws), extent[axis_at] // shards_of).reshape((-1,) + (1,) * (len(extent) - 1 - axis_at))
    return factor_of


def bell_draw(stream_key, extent, scale, limit, shards=(), dtype=jnp.bfloat16):
    drawn = jax.random.normal(stream_key, extent, jnp.float32) * scale
    if len(shards) > 0:
        drawn = shard_levels(stream_key, extent, shards, -0.22, 0.18) * drawn
    return jnp.clip(drawn, min=-limit, max=limit).astype(dtype)


def setup_inputs(seed: int = 0) -> dict:
    splits = jax.random.split(jax.random.key(seed), 7)
    return {
        "inputs": bell_draw(splits[0], (STEPS, DIN, TOKENS), 1.0, 6.0, ((1, 8), (2, 64))),
        "cotangent": bell_draw(splits[1], (STEPS, DOUT, TOKENS), 1.0, 6.0, ((1, 8), (2, 64))),
        "numerators": bell_draw(splits[2], (REPLICAS, DIN, DOUT), 1.0, 6.0, ((0, 64), (2, 8))),
        "momentum": bell_draw(splits[3], (REPLICAS, DIN, DOUT), 1.0, 6.0, ((0, 64), (2, 8))),
        "push_weight": jnp.clip(jnp.exp(math.log(2.0) - 1.3862944 * jax.random.uniform(splits[4], (REPLICAS,), jnp.float32) ** shard_levels(splits[4], (REPLICAS,), ((0, 64),), -0.2, 0.2)), 0.5, 2.0),
        "step_index": jax.random.randint(splits[5], (), 0, 1000).astype(jnp.int32),
    }


def head_backward(queries, upstream):
    rows = queries.shape[0]
    shaped = queries.reshape(rows // HEAD_DIM, HEAD_DIM, -1)
    upper = upstream.astype(jnp.float32).reshape(rows // HEAD_DIM, HEAD_DIM, -1)
    inverse = lax.rsqrt(lax.optimization_barrier(jnp.mean(shaped * shaped, axis=1, keepdims=True)) + 1e-06)
    normed = shaped * inverse
    inner = lax.optimization_barrier(jnp.mean(upper * normed, axis=1, keepdims=True))
    return (inverse * (upper - normed * inner)).reshape(rows, -1)

def replica_step(pieces):
    features, upstream, numerator, velocity, weight = pieces
    factor = DIN ** (-0.5)
    debiased = (numerator.astype(jnp.float32) / weight).astype(jnp.bfloat16)
    queries = factor * lax.dot_general(debiased, features, (((0,), (0,)), ((), ())), preferred_element_type=jnp.float32)
    query_grad = head_backward(queries, upstream).astype(jnp.bfloat16)
    width = DOUT // N_TENSOR
    blocks_w = debiased.astype(jnp.float32).reshape(DIN, N_TENSOR, width)
    blocks_g = query_grad.astype(jnp.float32).reshape(N_TENSOR, width, -1)
    partial_terms = factor * jnp.einsum('ajb,jbt->jat', blocks_w, blocks_g)
    rounded = lax.optimization_barrier(partial_terms.astype(jnp.bfloat16))
    grad_in = lax.optimization_barrier(jnp.sum(rounded.astype(jnp.float32), axis=0)).astype(jnp.bfloat16)
    grad_weight = factor * lax.dot_general(features, query_grad, (((1,), (1,)), ((), ())), preferred_element_type=jnp.float32)
    new_velocity = (0.9 * velocity.astype(jnp.float32) + grad_weight).astype(jnp.bfloat16)
    halfway = (numerator.astype(jnp.float32) - 0.25 * new_velocity.astype(jnp.float32)).astype(jnp.bfloat16)
    return (grad_in, new_velocity, lax.optimization_barrier(halfway))

def reference(inputs, cotangent, numerators, momentum, push_weight, step_index):
    levels = N_GOSSIP.bit_length() - 1
    numer_now = numerators
    velocity = momentum
    weights = push_weight
    grads_all = []
    for index in range(STEPS):
        features = inputs[index].reshape(DIN, N_GOSSIP, TOK).transpose(1, 0, 2)
        upstream = cotangent[index].reshape(DOUT, N_GOSSIP, TOK).transpose(1, 0, 2)
        grad_in, velocity, halfway = lax.map(replica_step, (features, upstream, numer_now, velocity, weights))
        power = ((step_index + index) % levels).astype(jnp.int32)
        distance = jnp.left_shift(jnp.int32(1), power)
        wide = halfway.astype(jnp.float32)
        numer_now = ((wide + jnp.roll(wide, distance, axis=0)) * 0.5).astype(jnp.bfloat16)
        weights = (weights + jnp.roll(weights, distance, axis=0)) * 0.5
        grads_all.append(grad_in.transpose(1, 0, 2).reshape(DIN, TOKENS))
    return (numer_now, velocity, weights, jnp.stack(grads_all))
```

```python
from functools import partial

import jax
import jax.numpy as jnp
from jax import lax
from jax.experimental import pallas as pl
from jax.experimental.pallas import tpu as pltpu
from jax.sharding import PartitionSpec as P

HEAD_DIM = 128
LEVELS = 6
PAD = 16
VMEM_LIMIT = 48 * 1024 * 1024

DIRECT = {k: ((2048, (k,)),) for k in (1, 2, 4, 8, 16, 32)}
HOPS8 = ((512, (4, 4)),) * 4
HOPS16 = ((512, (4, 4, 4, 4)),) * 4
BOTH16 = ((1536, (16,)), (512, (-24, -24)))


def plan_of(level):
    near, far = 1 << level, 1 << ((level + 1) % LEVELS)
    first = {8: HOPS8, 16: HOPS16}.get(near, DIRECT[near])
    second = {16: BOTH16}.get(far, DIRECT[far])
    return first, second


def passed_along(block, distance):
    count = lax.axis_size("gossip")
    route = [(i, (i + distance) % count) for i in range(count)]
    return lax.ppermute(block, "gossip", route)


def exchange(parts, plan):
    moved = list(parts)
    for leg in range(max(len(legs) for _, legs in plan)):
        moved = [
            passed_along(part, legs[leg]) if leg < len(legs) else part
            for part, (_, legs) in zip(moved, plan)
        ]
    return moved


def sizes_of(plan):
    sizes = [size for size, _ in plan]
    sizes[-1] += PAD
    return sizes


def whole(count):
    return [pl.BlockSpec(memory_space=pltpu.VMEM)] * count


def pieces(sizes, block):
    found = []
    at = 0
    for part, size in enumerate(sizes):
        for row in range(0, size, block):
            found.append((part, row, at + row))
        at += size
    return found


def head_backward(queries, upstream):
    results = []
    for start in range(0, queries.shape[1], HEAD_DIM):
        q = queries[:, start : start + HEAD_DIM]
        upper = upstream[:, start : start + HEAD_DIM].astype(jnp.float32)
        inverse = lax.rsqrt(jnp.mean(q * q, axis=1, keepdims=True) + 1e-06)
        normed = q * inverse
        inner = jnp.mean(upper * normed, axis=1, keepdims=True)
        results.append(inverse * (upper - normed * inner))
    return jnp.concatenate(results, axis=1)


def step_kernel(factor, averaged, sizes_in, sizes_out, *refs):
    take = iter(refs)
    weight_ref = next(take)
    own = [next(take) for _ in sizes_in]
    came = [next(take) for _ in sizes_in] if averaged else None
    feature_ref, upstream_ref, velocity_ref = next(take), next(take), next(take)
    halfway = [next(take) for _ in sizes_out]
    velocity_out, debiased_ref, grad_ref = next(take), next(take), next(take)
    numer_ref = next(take) if averaged else None
    block = feature_ref.shape[2]
    tail = sizes_in[-1]
    if averaged:
        extra = came[-1][pl.ds(tail, PAD), :].astype(jnp.float32)
        mine = own[-1][pl.ds(tail, PAD), :].astype(jnp.float32)
        weight = (mine[0:1] + mine[1:2] + (extra[0:1] + extra[1:2])) * 0.5
    else:
        weight = jnp.full((1, block), weight_ref[0], jnp.float32)
    scale = 1.0 / weight
    total = None
    for j, (part, row, _) in enumerate(pieces(sizes_in, block)):
        rows = pl.ds(row, block)
        numer = own[part][rows, :].astype(jnp.float32)
        if averaged:
            numer = ((numer + came[part][rows, :].astype(jnp.float32)) * 0.5).astype(jnp.bfloat16)
            numer_ref[pl.ds(j * block, block), :] = numer
            numer = numer.astype(jnp.float32)
        debiased = (numer * scale).astype(jnp.bfloat16)
        debiased_ref[pl.ds(j * block, block), :] = debiased
        term = jnp.dot(feature_ref[j], debiased, preferred_element_type=jnp.float32)
        total = term if total is None else total + term
    grad = head_backward(factor * total, upstream_ref[...]).astype(jnp.bfloat16)
    grad_ref[...] = grad
    places = {at: (part, row) for part, row, at in pieces(sizes_in, block)}
    for j, (part, row, at) in enumerate(pieces(sizes_out, block)):
        rows = pl.ds(at, block)
        grad_weight = factor * lax.dot_general(
            feature_ref[j], grad, (((0,), (0,)), ((), ())), preferred_element_type=jnp.float32
        )
        velocity = (0.9 * velocity_ref[rows, :].astype(jnp.float32) + grad_weight).astype(
            jnp.bfloat16
        )
        velocity_out[rows, :] = velocity
        if averaged:
            numer = numer_ref[rows, :]
        else:
            part_in, row_in = places[at]
            numer = own[part_in][pl.ds(row_in, block), :]
        half = numer.astype(jnp.float32) - 0.25 * velocity.astype(jnp.float32)
        halfway[part][pl.ds(row, block), :] = half.astype(jnp.bfloat16)
    high = weight.astype(jnp.bfloat16).astype(jnp.float32)
    line = lax.broadcasted_iota(jnp.int32, (PAD, block), 0)
    rest = jnp.where(line == 0, high, jnp.where(line == 1, weight - high, 0.0))
    halfway[-1][pl.ds(sizes_out[-1], PAD), :] = rest.astype(jnp.bfloat16)


def step(weight, own, came, sizes_in, plan_out, features, upstream, velocity, factor):
    rows, width = velocity.shape
    tokens = upstream.shape[0]
    averaged = came is not None
    sizes = [size for size, _ in plan_out]
    bf16 = jnp.bfloat16
    out_shape = [jax.ShapeDtypeStruct((n, width), bf16) for n in sizes_of(plan_out)]
    out_shape += [
        jax.ShapeDtypeStruct((rows, width), bf16),
        jax.ShapeDtypeStruct((rows, width), bf16),
        jax.ShapeDtypeStruct((tokens, width), bf16),
    ]
    operands = [*own, *(came or []), features, upstream, velocity]
    results = pl.pallas_call(
        partial(step_kernel, factor, averaged, sizes_in, sizes),
        out_shape=out_shape,
        in_specs=[pl.BlockSpec(memory_space=pltpu.SMEM)] + whole(len(operands)),
        out_specs=whole(len(out_shape)),
        scratch_shapes=[pltpu.VMEM((rows, width), bf16)] if averaged else [],
        compiler_params=pltpu.CompilerParams(vmem_limit_bytes=VMEM_LIMIT),
        cost_estimate=pl.CostEstimate(
            flops=4 * rows * width * tokens, bytes_accessed=8 << 20, transcendentals=0
        ),
        name="optimizer_step",
    )(weight, *operands)
    return results[: len(sizes)], *results[len(sizes) :]


def term_kernel(factor, debiased_ref, grad_ref, out_ref):
    block = out_ref.shape[2]
    for j in range(out_ref.shape[0]):
        part = lax.dot_general(
            grad_ref[...],
            debiased_ref[pl.ds(j * block, block), :],
            (((1,), (1,)), ((), ())),
            preferred_element_type=jnp.float32,
        )
        out_ref[j] = (factor * part).astype(jnp.bfloat16)


def input_terms(debiased, grad, factor):
    rows, width = debiased.shape
    tokens = grad.shape[0]
    return pl.pallas_call(
        partial(term_kernel, factor),
        out_shape=jax.ShapeDtypeStruct((rows // width, tokens, width), jnp.bfloat16),
        in_specs=whole(2),
        out_specs=whole(1)[0],
        compiler_params=pltpu.CompilerParams(vmem_limit_bytes=VMEM_LIMIT),
        cost_estimate=pl.CostEstimate(
            flops=2 * rows * width * tokens, bytes_accessed=3 << 20, transcendentals=0
        ),
        name="input_terms",
    )(debiased, grad)


def sum_kernel(in_ref, out_ref):
    total = in_ref[0].astype(jnp.float32)
    for j in range(1, in_ref.shape[0]):
        total = total + in_ref[j].astype(jnp.float32)
    out_ref[...] = total.astype(jnp.bfloat16)


def input_gradient(debiased, grad, factor, offload):
    terms = input_terms(debiased, grad, factor)
    count, tokens, width = terms.shape
    if offload:
        return lax.psum_scatter(
            terms.reshape(count * tokens, width), "tensor", scatter_dimension=0, tiled=True
        )
    swapped = lax.all_to_all(terms, "tensor", 0, 0)
    return pl.pallas_call(
        sum_kernel,
        out_shape=jax.ShapeDtypeStruct((tokens, width), jnp.bfloat16),
        in_specs=whole(1),
        out_specs=whole(1)[0],
        compiler_params=pltpu.CompilerParams(vmem_limit_bytes=VMEM_LIMIT),
        name="sum_terms",
    )(swapped)


def final_kernel(sizes, *refs):
    count = len(sizes)
    own, came = refs[:count], refs[count : 2 * count]
    numer_ref, weight_ref = refs[2 * count :]
    at = 0
    for part, size in enumerate(sizes):
        both = own[part][pl.ds(0, size), :].astype(jnp.float32) + came[part][
            pl.ds(0, size), :
        ].astype(jnp.float32)
        numer_ref[pl.ds(at, size), :] = (both * 0.5).astype(jnp.bfloat16)
        at += size
    mine = own[-1][pl.ds(sizes[-1], PAD), :].astype(jnp.float32)
    extra = came[-1][pl.ds(sizes[-1], PAD), :].astype(jnp.float32)
    weight = (mine[0:1] + mine[1:2] + (extra[0:1] + extra[1:2])) * 0.5
    weight_ref[...] = jnp.broadcast_to(weight, weight_ref.shape)


def final_average(own, came, plan):
    sizes = [size for size, _ in plan]
    width = own[0].shape[1]
    return pl.pallas_call(
        partial(final_kernel, sizes),
        out_shape=[
            jax.ShapeDtypeStruct((sum(sizes), width), jnp.bfloat16),
            jax.ShapeDtypeStruct((8, width), jnp.float32),
        ],
        in_specs=whole(2 * len(sizes)),
        out_specs=whole(2),
        compiler_params=pltpu.CompilerParams(vmem_limit_bytes=VMEM_LIMIT),
        name="final_average",
    )(*own, *came)


def two_steps(level, inputs, cotangent, numerators, momentum, push_weight):
    first, second = plan_of(level)
    near = 1 << level
    tensors = lax.axis_size("tensor")
    factor = (inputs.shape[2] * tensors) ** (-0.5)
    whole_plan = DIRECT[1]
    spread = jnp.broadcast_to(inputs[0][None], (tensors, *inputs.shape[1:]))
    features = lax.all_to_all(spread, "tensor", 0, 0)
    later = lax.all_gather(inputs[1], "tensor", axis=0)
    numer = numerators[0]
    half, velocity, debiased, grad = step(
        push_weight, [numer], None, [2048], first, features, cotangent[0], momentum[0], factor
    )
    came = exchange(half, first)
    grad_in_0 = input_gradient(debiased, grad, factor, offload=near in (8, 16))
    half2, velocity, debiased, grad = step(
        push_weight,
        half,
        came,
        [size for size, _ in first],
        second,
        later,
        cotangent[1],
        velocity,
        factor,
    )
    came2 = exchange(half2, second)
    grad_in_1 = input_gradient(debiased, grad, factor, offload=False)
    numer, weight = final_average(half2, came2, second)
    return numer[None], velocity[None], weight[0, :1], jnp.stack([grad_in_0, grad_in_1])


def body(inputs, cotangent, numerators, momentum, push_weight, step_index):
    inputs = inputs.transpose(0, 2, 1)
    cotangent = cotangent.transpose(0, 2, 1)
    numer, velocity, weight, grads = lax.switch(
        lax.rem(step_index, LEVELS),
        [partial(two_steps, level) for level in range(LEVELS)],
        inputs,
        cotangent,
        numerators,
        momentum,
        push_weight,
    )
    return numer, velocity, weight, grads.transpose(0, 2, 1)


def solution(mesh):
    placed = (
        P(None, "tensor", "gossip"),
        P(None, "tensor", "gossip"),
        P("gossip", None, "tensor"),
        P("gossip", None, "tensor"),
        P("gossip"),
        P(),
    )
    return jax.shard_map(
        body,
        mesh=mesh,
        in_specs=placed,
        out_specs=(
            P("gossip", None, "tensor"),
            P("gossip", None, "tensor"),
            P("gossip"),
            P(None, "tensor", "gossip"),
        ),
        check_vma=False,
    )
```

```python
from functools import partial

import jax
import jax.numpy as jnp
from jax import lax
from jax.experimental import pallas as pl
from jax.experimental.pallas import tpu as pltpu
from jax.sharding import PartitionSpec as P

HEAD_DIM = 128
LEVELS = 6
PAD = 16
VMEM_LIMIT = 16 * 1024 * 1024
BF16 = jnp.bfloat16
VMEM = pl.BlockSpec(memory_space=pltpu.VMEM)
SMEM = pl.BlockSpec(memory_space=pltpu.SMEM)

CUTS = {
    "plain": lambda k: ((2048, (k,)),),
    "hops": lambda k: ((512, (4,) * (k // 4)),) * 4,
    "both": lambda k: ((1536, (k,)), (512, (-24, -24))),
}
LEVEL_PLANS = (
    ("plain", "plain", "apart", False),
    ("plain", "plain", "apart", True),
    ("plain", "plain", "late", False),
    ("hops", "both", "joined", False),
    ("hops", "plain", "joined", False),
    ("plain", "plain", "joined", False),
)


def passed_along(block, distance):
    count = lax.axis_size("gossip")
    route = [(i, (i + distance) % count) for i in range(count)]
    return lax.ppermute(block, "gossip", route)


def swapped_pair(block):
    count = lax.axis_size("tensor")
    return lax.ppermute(block, "tensor", [(i, i ^ 1) for i in range(count)])


def along_x(blocks):
    count = lax.axis_size("tensor")
    groups = [list(range(y, count, 2)) for y in range(2)]
    return lax.all_to_all(blocks, "tensor", 0, 0, axis_index_groups=groups)


def exchange(half, plan):
    parts, at = [], 0
    for number, (size, _) in enumerate(plan):
        size += PAD if number == len(plan) - 1 else 0
        parts.append(half if len(plan) == 1 else half[at : at + size])
        at += size
    for leg in range(max(len(legs) for _, legs in plan)):
        parts = [
            passed_along(part, legs[leg]) if leg < len(legs) else part
            for part, (_, legs) in zip(parts, plan)
        ]
    return parts


def call(kernel, out_shape, operands, name, cost=(0, 1 << 20), in_specs=None, out_specs=None, scratch=()):
    return pl.pallas_call(
        kernel,
        out_shape=out_shape,
        in_specs=in_specs or [VMEM] * len(operands),
        out_specs=out_specs or [VMEM] * len(out_shape),
        scratch_shapes=scratch,
        compiler_params=pltpu.CompilerParams(vmem_limit_bytes=VMEM_LIMIT),
        cost_estimate=pl.CostEstimate(flops=cost[0], bytes_accessed=cost[1], transcendentals=0),
        name=name,
    )(*operands)


def spread_kernel(inputs_ref, now_ref, later_ref):
    first = inputs_ref[0]
    for j in range(now_ref.shape[0]):
        now_ref[j, 0] = first
    later_ref[...] = inputs_ref[1]


def spread(inputs, count):
    _, tokens, width = inputs.shape
    many = jax.ShapeDtypeStruct((count, 1, tokens, width), BF16)
    one = jax.ShapeDtypeStruct((tokens, width), BF16)
    return call(spread_kernel, [many, one], [inputs], "spread")


def spread_pair_kernel(mine_ref, other_ref, spread_ref):
    here = lax.rem(lax.axis_index("tensor"), 2) == 0
    mine, other = mine_ref[...], other_ref[...]
    low = jnp.where(here, mine, other)
    high = jnp.where(here, other, mine)
    for x in range(spread_ref.shape[0]):
        spread_ref[x, 0] = low
        spread_ref[x, 1] = high


def spread_pair(mine, other, count):
    return call(
        spread_pair_kernel,
        [jax.ShapeDtypeStruct((count, 2, *mine.shape), BF16)],
        [mine, other],
        "spread_pair",
    )[0]


def head_backward(queries, upstream):
    results = []
    for start in range(0, queries.shape[1], HEAD_DIM):
        q = queries[:, start : start + HEAD_DIM]
        upper = upstream[:, start : start + HEAD_DIM].astype(jnp.float32)
        inverse = lax.rsqrt(jnp.mean(q * q, axis=1, keepdims=True) + 1e-06)
        normed = q * inverse
        inner = jnp.mean(upper * normed, axis=1, keepdims=True)
        results.append(inverse * (upper - normed * inner))
    return jnp.concatenate(results, axis=1)


def repeat(count, unroll, one):
    if unroll >= count:
        for j in range(count):
            one(j)
        return

    def several(turn, carry):
        for k in range(unroll):
            one(turn * unroll + k)
        return carry

    lax.fori_loop(0, count // unroll, several, 0)


def block_rows(j, block):
    return pl.ds(j * block if isinstance(j, int) else pl.multiple_of(j * block, block), block)


def step_kernel(
    factor, index, unroll, weight_ref, numer, features, upstream, momentum,
    half_out, momentum_out, debiased_out, grad_out, total,
):
    count, block = features.shape[0], features.shape[3]
    weight = jnp.full((1, block), weight_ref[0], jnp.float32)
    scale = 1.0 / weight
    total[...] = jnp.zeros_like(total)

    def query_term(j):
        rows = block_rows(j, block)
        divided = (numer[rows, :].astype(jnp.float32) * scale).astype(BF16)
        debiased_out[rows, :] = divided
        total[...] += jnp.dot(features[j, 0], divided, preferred_element_type=jnp.float32)

    repeat(count, unroll, query_term)
    grad = head_backward(factor * total[...], upstream[index]).astype(BF16)
    grad_out[...] = grad

    def update(j):
        rows = block_rows(j, block)
        grad_weight = factor * lax.dot_general(
            features[j, 0], grad_out[...], (((0,), (0,)), ((), ())), preferred_element_type=jnp.float32
        )
        moved = (0.9 * momentum[rows, :].astype(jnp.float32) + grad_weight).astype(BF16)
        momentum_out[rows, :] = moved
        held = numer[rows, :].astype(jnp.float32)
        half_out[rows, :] = (held - 0.25 * moved.astype(jnp.float32)).astype(BF16)

    repeat(count, unroll, update)
    high = weight.astype(BF16).astype(jnp.float32)
    line = lax.broadcasted_iota(jnp.int32, (PAD, block), 0)
    lines = jnp.where(line == 0, high, jnp.where(line == 1, weight - high, 0.0))
    half_out[pl.ds(count * block, PAD), :] = lines.astype(BF16)


def step(index, unroll, weight, numer, features, cotangent, momentum, factor):
    rows, width = momentum.shape
    tokens = cotangent.shape[1]
    operands = [weight, numer, features, cotangent, momentum]
    return call(
        partial(step_kernel, factor, index, unroll),
        [jax.ShapeDtypeStruct((n, width), BF16) for n in (rows + PAD, rows, rows, tokens)],
        operands,
        "optimizer_step",
        (4 * rows * width * tokens, 8 << 20),
        [SMEM] + [VMEM] * 4,
        scratch=[pltpu.VMEM((tokens, width), jnp.float32)],
    )


def average_kernel(sizes, own, *refs):
    came, numer, weight = refs[:-2], refs[-2], refs[-1]
    at, block = 0, 64
    for part, size in zip(came, sizes):

        def one(j, part=part, at=at):
            here = pl.ds(pl.multiple_of(at + j * block, block), block)
            both = own[here, :].astype(jnp.float32)
            both = both + part[pl.ds(pl.multiple_of(j * block, block), block), :].astype(jnp.float32)
            numer[here, :] = (both * 0.5).astype(BF16)

        repeat(size // block, 4, one)
        at += size
    mine = own[pl.ds(at, PAD), :].astype(jnp.float32)
    other = came[-1][pl.ds(sizes[-1], PAD), :].astype(jnp.float32)
    weight[0] = jnp.max((mine[0:1] + mine[1:2] + (other[0:1] + other[1:2])) * 0.5)


def average(own, came, plan):
    rows, width = own.shape[0] - PAD, own.shape[1]
    return call(
        partial(average_kernel, [size for size, _ in plan]),
        [jax.ShapeDtypeStruct((rows, width), BF16), jax.ShapeDtypeStruct((1,), jnp.float32)],
        [own, *came],
        "average",
        (1 << 50, 1 << 40),
        out_specs=[VMEM, SMEM],
    )


def blocks_kernel(factor, kept, *refs):
    out = refs[-1]
    count, block = out.shape[0], out.shape[3]
    for slot in range(kept):
        value = refs[slot][...]
        for j in range(count):
            out[j, slot] = value
    pairs = refs[kept:-1]

    def one(j):
        for number in range(len(pairs) // 2):
            debiased, grad = pairs[2 * number], pairs[2 * number + 1]
            part = lax.dot_general(
                grad[...],
                debiased[block_rows(j, block), :],
                (((1,), (1,)), ((), ())),
                preferred_element_type=jnp.float32,
            )
            out[j, kept + number] = (factor * part).astype(BF16)

    if pairs:
        repeat(count, 2, one)


def blocks_for_peers(factor, kept, pairs):
    tokens, width = (kept or pairs[0][1:])[0].shape
    count = lax.axis_size("tensor")
    operands = [*kept, *(ref for pair in pairs for ref in pair)]
    return call(
        partial(blocks_kernel, factor, len(kept)),
        [jax.ShapeDtypeStruct((count, len(kept) + len(pairs), tokens, width), BF16)],
        operands,
        "blocks_for_peers",
        (2 * len(pairs) * count * width * width * tokens, 3 << 20),
    )[0]


def total_of(ref, places):
    total = None
    for place in places:
        term = ref[place].astype(jnp.float32)
        total = term if total is None else total + term
    return total


def add_kernel(mine_ref, came_ref, out_ref):
    out_ref[...] = (mine_ref[...] + came_ref[...].astype(jnp.float32)).astype(BF16)


def pair_kernel(in_ref, mine_ref, other_ref):
    count = in_ref.shape[0]
    sums = [total_of(in_ref, [(x, y) for x in range(count)]) for y in range(2)]
    here = lax.rem(lax.axis_index("tensor"), 2) == 0
    mine_ref[...] = jnp.where(here, sums[0], sums[1])
    other_ref[...] = jnp.where(here, sums[1], sums[0]).astype(BF16)


def sum_kernel(slot, in_ref, out_ref):
    out_ref[...] = total_of(in_ref, [(j, slot) for j in range(in_ref.shape[0])]).astype(BF16)


def collect_kernel(slots, first_ref, second_ref, out_ref):
    for index, (slot, ref) in enumerate(zip(slots, (first_ref, second_ref))):
        if slot is None:
            out_ref[index] = ref[...]
        else:
            places = [(j, slot) for j in range(ref.shape[0])]
            out_ref[index] = total_of(ref, places).astype(BF16)


def swapped_all(blocks):
    return lax.all_to_all(blocks, "tensor", 0, 0)


def first_sum(swapped, kind):
    shape = swapped.shape[-2:]
    result = [jax.ShapeDtypeStruct(shape, BF16)]
    if kind == "joined":
        return call(partial(sum_kernel, 1), result, [swapped], "sum_terms")[0]
    mine, other = call(
        pair_kernel, [jax.ShapeDtypeStruct(shape, jnp.float32), *result], [swapped], "sum_pair"
    )
    return call(add_kernel, result, [mine, swapped_pair(other)], "add_pair")[0]


def after_first_half(level, factor, half, velocity, debiased, grad, later, cotangent):
    first, second, kind, x_gather = LEVEL_PLANS[level]
    first = CUTS[first](1 << level)
    second = CUTS[second](1 << ((level + 1) % LEVELS))
    shape, count = later.shape, lax.axis_size("tensor")
    came = exchange(half, first)
    if x_gather:
        pairs = spread_pair(later, swapped_pair(later), count // 2)
        features = along_x(pairs).reshape(count, 1, *shape)
    else:
        terms = [(debiased, grad)] if kind == "joined" else []
        features = swapped_all(blocks_for_peers(factor, [later], terms))
    if kind == "apart":
        terms = blocks_for_peers(factor, [], [(debiased, grad)])
        swapped = along_x(terms.reshape(count // 2, 2, *shape))
    else:
        swapped = features
    numer, weight = average(half, came, first)
    half, velocity, debiased_2, grad_2 = step(
        1, 4, weight, numer, features, cotangent, velocity, factor
    )
    came = exchange(half, second)
    terms = [(debiased_2, grad_2)]
    if kind == "late":
        terms.insert(0, (debiased, grad))
    else:
        grad_in = first_sum(swapped, kind)
    swapped = swapped_all(blocks_for_peers(factor, [], terms))
    numer, weight = average(half, came, second)
    swapped, numer = lax.optimization_barrier((swapped, numer))
    slots, parts = ((0, 1), [swapped] * 2) if kind == "late" else ((None, 0), [grad_in, swapped])
    grads = call(
        partial(collect_kernel, slots),
        [jax.ShapeDtypeStruct((2, *shape), BF16)],
        parts,
        "collect",
    )[0]
    return numer, velocity, weight, grads


def body(inputs, cotangent, numerators, momentum, push_weight, step_index):
    inputs, cotangent = inputs.transpose(0, 2, 1), cotangent.transpose(0, 2, 1)
    tensors = lax.axis_size("tensor")
    factor = (inputs.shape[2] * tensors) ** (-0.5)
    now, later = spread(inputs, tensors)
    half, velocity, debiased, grad = step(
        0, tensors, push_weight, numerators[0], swapped_all(now), cotangent, momentum[0], factor
    )
    numer, velocity, weight, grads = lax.switch(
        lax.rem(step_index, LEVELS),
        [partial(after_first_half, level, factor) for level in range(LEVELS)],
        half,
        velocity,
        debiased,
        grad,
        later,
        cotangent,
    )
    return numer[None], velocity[None], weight, grads.transpose(0, 2, 1)


def solution(mesh):
    placed = (
        P(None, "tensor", "gossip"),
        P(None, "tensor", "gossip"),
        P("gossip", None, "tensor"),
        P("gossip", None, "tensor"),
        P("gossip"),
        P(),
    )
    return jax.shard_map(
        body,
        mesh=mesh,
        in_specs=placed,
        out_specs=(
            P("gossip", None, "tensor"),
            P("gossip", None, "tensor"),
            P("gossip"),
            P(None, "tensor", "gossip"),
        ),
        check_vma=False,
    )
```

```python
from functools import partial

import jax
import jax.numpy as jnp
from jax import lax
from jax.experimental import pallas as pl
from jax.experimental.pallas import tpu as pltpu
from jax.sharding import PartitionSpec as P

HEAD_DIM = 128
LEVELS = 6
PAD = 16
VMEM_LIMIT = 16 * 1024 * 1024
BF16 = jnp.bfloat16
VMEM = pl.BlockSpec(memory_space=pltpu.VMEM)
SMEM = pl.BlockSpec(memory_space=pltpu.SMEM)
HBM = pl.BlockSpec(memory_space=pltpu.HBM)

CUTS = {
    "plain": lambda k: ((2048, (k,)),),
    "hops": lambda k: ((512, (4,) * (k // 4)),) * 4,
    "both": lambda k: ((1664, (k,)), (384, (-24, -24))),
}
LEVEL_PLANS = (
    ("plain", "plain", "late", False, True),
    ("plain", "plain", "late", True, False),
    ("plain", "plain", "late", False, False),
    ("hops", "both", "late", False, False),
    ("hops", "plain", "late", False, False),
    ("plain", "plain", "joined", False, False),
)


def passed_along(block, distance):
    count = lax.axis_size("gossip")
    route = [(i, (i + distance) % count) for i in range(count)]
    return lax.ppermute(block, "gossip", route)


def swapped_pair(block):
    count = lax.axis_size("tensor")
    return lax.ppermute(block, "tensor", [(i, i ^ 1) for i in range(count)])


def along_x(blocks):
    count = lax.axis_size("tensor")
    groups = [list(range(y, count, 2)) for y in range(2)]
    return lax.all_to_all(blocks, "tensor", 0, 0, axis_index_groups=groups)


def exchange(half, plan):
    parts, at = [], 0
    for number, (size, _) in enumerate(plan):
        size += PAD if number == len(plan) - 1 else 0
        parts.append(half if len(plan) == 1 else half[at : at + size])
        at += size
    for leg in range(max(len(legs) for _, legs in plan)):
        parts = [
            passed_along(part, legs[leg]) if leg < len(legs) else part
            for part, (_, legs) in zip(parts, plan)
        ]
    return parts


def call(kernel, out_shape, operands, name, cost=(0, 1 << 20), in_specs=None, out_specs=None, scratch=()):
    return pl.pallas_call(
        kernel,
        out_shape=out_shape,
        in_specs=in_specs or [VMEM] * len(operands),
        out_specs=out_specs or [VMEM] * len(out_shape),
        scratch_shapes=scratch,
        compiler_params=pltpu.CompilerParams(vmem_limit_bytes=VMEM_LIMIT),
        cost_estimate=pl.CostEstimate(flops=cost[0], bytes_accessed=cost[1], transcendentals=0),
        name=name,
    )(*operands)


def spread_kernel(inputs_ref, now_ref, first, semaphore):
    load = pltpu.make_async_copy(inputs_ref.at[0], first, semaphore)
    load.start()
    load.wait()
    value = first[...]
    for j in range(now_ref.shape[0]):
        now_ref[j, 0] = value


def spread(inputs, count):
    block = inputs.shape[1:]
    return call(
        spread_kernel,
        [jax.ShapeDtypeStruct((count, 1, *block), BF16)],
        [inputs],
        "spread",
        in_specs=[HBM],
        scratch=[pltpu.VMEM(block, BF16), pltpu.SemaphoreType.DMA],
    )[0]


def spread_pair_kernel(mine_ref, other_ref, spread_ref):
    here = lax.rem(lax.axis_index("tensor"), 2) == 0
    mine, other = mine_ref[...], other_ref[...]
    low = jnp.where(here, mine, other)
    high = jnp.where(here, other, mine)
    for x in range(spread_ref.shape[0]):
        spread_ref[x, 0] = low
        spread_ref[x, 1] = high


def spread_pair(mine, other, count):
    return call(
        spread_pair_kernel,
        [jax.ShapeDtypeStruct((count, 2, *mine.shape), BF16)],
        [mine, other],
        "spread_pair",
    )[0]


def head_backward(queries, upstream):
    results = []
    for start in range(0, queries.shape[1], HEAD_DIM):
        q = queries[:, start : start + HEAD_DIM]
        upper = upstream[:, start : start + HEAD_DIM].astype(jnp.float32)
        inverse = lax.rsqrt(jnp.mean(q * q, axis=1, keepdims=True) + 1e-06)
        normed = q * inverse
        inner = jnp.mean(upper * normed, axis=1, keepdims=True)
        results.append(inverse * (upper - normed * inner))
    return jnp.concatenate(results, axis=1)


def repeat(count, unroll, one):
    if unroll >= count:
        for j in range(count):
            one(j)
        return

    def several(turn, carry):
        for k in range(unroll):
            one(turn * unroll + k)
        return carry

    lax.fori_loop(0, count // unroll, several, 0)


def block_rows(j, block):
    return pl.ds(j * block if isinstance(j, int) else pl.multiple_of(j * block, block), block)


def step_kernel(
    factor, index, unroll, weight_ref, numer, features, upstream, momentum,
    half_out, momentum_out, debiased_out, grad_out, total,
):
    count, block = features.shape[0], features.shape[3]
    weight = jnp.full((1, block), weight_ref[0], jnp.float32)
    scale = 1.0 / weight
    total[...] = jnp.zeros_like(total)

    def query_term(j):
        rows = block_rows(j, block)
        divided = (numer[rows, :].astype(jnp.float32) * scale).astype(BF16)
        debiased_out[rows, :] = divided
        total[...] += jnp.dot(features[j, 0], divided, preferred_element_type=jnp.float32)

    repeat(count, unroll, query_term)
    grad = head_backward(factor * total[...], upstream[index]).astype(BF16)
    grad_out[...] = grad

    def update(j):
        rows = block_rows(j, block)
        grad_weight = factor * lax.dot_general(
            features[j, 0], grad_out[...], (((0,), (0,)), ((), ())), preferred_element_type=jnp.float32
        )
        moved = (0.9 * momentum[rows, :].astype(jnp.float32) + grad_weight).astype(BF16)
        momentum_out[rows, :] = moved
        held = numer[rows, :].astype(jnp.float32)
        half_out[rows, :] = (held - 0.25 * moved.astype(jnp.float32)).astype(BF16)

    repeat(count, unroll, update)
    high = weight.astype(BF16).astype(jnp.float32)
    line = lax.broadcasted_iota(jnp.int32, (PAD, block), 0)
    lines = jnp.where(line == 0, high, jnp.where(line == 1, weight - high, 0.0))
    half_out[pl.ds(count * block, PAD), :] = lines.astype(BF16)


def step(index, unroll, weight, numer, features, cotangent, momentum, factor):
    rows, width = momentum.shape
    tokens = cotangent.shape[1]
    operands = [weight, numer, features, cotangent, momentum]
    return call(
        partial(step_kernel, factor, index, unroll),
        [jax.ShapeDtypeStruct((n, width), BF16) for n in (rows + PAD, rows, rows, tokens)],
        operands,
        "optimizer_step",
        (4 * rows * width * tokens, 8 << 20),
        [SMEM] + [VMEM] * 4,
        scratch=[pltpu.VMEM((tokens, width), jnp.float32)],
    )


def average_kernel(sizes, own, *refs):
    came, numer, weight = refs[:-2], refs[-2], refs[-1]
    at, block = 0, 64
    for part, size in zip(came, sizes):

        def one(j, part=part, at=at):
            here = pl.ds(pl.multiple_of(at + j * block, block), block)
            both = own[here, :].astype(jnp.float32)
            both = both + part[pl.ds(pl.multiple_of(j * block, block), block), :].astype(jnp.float32)
            numer[here, :] = (both * 0.5).astype(BF16)

        repeat(size // block, 2, one)
        at += size
    mine = own[pl.ds(at, PAD), :].astype(jnp.float32)
    other = came[-1][pl.ds(sizes[-1], PAD), :].astype(jnp.float32)
    weight[0] = jnp.max((mine[0:1] + mine[1:2] + (other[0:1] + other[1:2])) * 0.5)


def average(own, came, plan, cost):
    rows, width = own.shape[0] - PAD, own.shape[1]
    return call(
        partial(average_kernel, [size for size, _ in plan]),
        [jax.ShapeDtypeStruct((rows, width), BF16), jax.ShapeDtypeStruct((1,), jnp.float32)],
        [own, *came],
        "average",
        (1 << cost, 1 << 20),
        out_specs=[VMEM, SMEM],
    )


def blocks_kernel(factor, kept, *refs):
    out = refs[-1]
    count, block = out.shape[0], out.shape[3]
    for slot in range(kept):
        value = refs[slot][...]
        for j in range(count):
            out[j, slot] = value
    pairs = refs[kept:-1]

    def one(j):
        for number in range(len(pairs) // 2):
            debiased, grad = pairs[2 * number], pairs[2 * number + 1]
            part = lax.dot_general(
                grad[...],
                debiased[block_rows(j, block), :],
                (((1,), (1,)), ((), ())),
                preferred_element_type=jnp.float32,
            )
            out[j, kept + number] = (factor * part).astype(BF16)

    if pairs:
        repeat(count, 2, one)


def blocks_for_peers(factor, kept, pairs):
    tokens, width = (kept or pairs[0][1:])[0].shape
    count = lax.axis_size("tensor")
    operands = [*kept, *(ref for pair in pairs for ref in pair)]
    return call(
        partial(blocks_kernel, factor, len(kept)),
        [jax.ShapeDtypeStruct((count, len(kept) + len(pairs), tokens, width), BF16)],
        operands,
        "blocks_for_peers",
        (2 * len(pairs) * count * width * width * tokens, 3 << 20),
    )[0]


def total_of(ref, places):
    total = None
    for place in places:
        term = ref[place].astype(jnp.float32)
        total = term if total is None else total + term
    return total


def add_kernel(mine_ref, came_ref, out_ref):
    out_ref[...] = (mine_ref[...] + came_ref[...].astype(jnp.float32)).astype(BF16)


def pair_kernel(in_ref, mine_ref, other_ref):
    count = in_ref.shape[0]
    here = lax.rem(lax.axis_index("tensor"), 2) == 0
    for slot in range(in_ref.shape[2]):
        low, high = (total_of(in_ref, [(x, y, slot) for x in range(count)]) for y in range(2))
        mine_ref[slot] = jnp.where(here, low, high)
        other_ref[slot] = jnp.where(here, high, low).astype(BF16)


def sum_kernel(slot, in_ref, out_ref):
    out_ref[...] = total_of(in_ref, [(j, slot) for j in range(in_ref.shape[0])]).astype(BF16)


def collect_kernel(slots, first_ref, second_ref, out_ref):
    for index, (slot, ref) in enumerate(zip(slots, (first_ref, second_ref))):
        if slot is None:
            out_ref[index] = ref[...]
        else:
            places = [(j, slot) for j in range(ref.shape[0])]
            out_ref[index] = total_of(ref, places).astype(BF16)


def swapped_all(blocks):
    return lax.all_to_all(blocks, "tensor", 0, 0)


def after_first_half(level, factor, half, velocity, debiased, grad, later, cotangent):
    first, second, kind, x_gather, x_sum = LEVEL_PLANS[level]
    first = CUTS[first](1 << level)
    second = CUTS[second](1 << ((level + 1) % LEVELS))
    shape, count = later.shape, lax.axis_size("tensor")
    one, both = jax.ShapeDtypeStruct(shape, BF16), jax.ShapeDtypeStruct((2, *shape), BF16)
    if x_gather:
        half, other = lax.optimization_barrier((half, swapped_pair(later)))
        pairs = spread_pair(later, other, count // 2)
        features = along_x(pairs).reshape(count, 1, *shape)
    else:
        terms = [(debiased, grad)] if kind == "joined" else []
        features = swapped_all(blocks_for_peers(factor, [later], terms))
    came = exchange(half, first)
    numer, weight = average(half, came, first, 35 if kind == "joined" else 33)
    half, velocity, debiased_2, grad_2 = step(
        1, 4, weight, numer, features, cotangent, velocity, factor
    )
    came = exchange(half, second)
    terms = [(debiased_2, grad_2)]
    if kind == "late":
        terms.insert(0, (debiased, grad))
    else:
        grad_in = call(partial(sum_kernel, 1), [one], [features], "sum_terms")[0]
    blocks = blocks_for_peers(factor, [], terms)
    if x_sum:
        swapped = along_x(blocks.reshape(count // 2, 2, *blocks.shape[1:]))
    else:
        swapped = swapped_all(blocks)
    numer, weight = average(half, came, second, 35)
    swapped, numer = lax.optimization_barrier((swapped, numer))
    if x_sum:
        wide = jax.ShapeDtypeStruct(both.shape, jnp.float32)
        mine, other = call(pair_kernel, [wide, both], [swapped], "sum_pair")
        grads = call(add_kernel, [both], [mine, swapped_pair(other)], "add_pair")[0]
    else:
        slots, parts = ((0, 1), [swapped] * 2) if kind == "late" else ((None, 0), [grad_in, swapped])
        grads = call(partial(collect_kernel, slots), [both], parts, "collect")[0]
    return numer, velocity, weight, grads


def body(inputs, cotangent, numerators, momentum, push_weight, step_index):
    inputs, cotangent = inputs.transpose(0, 2, 1), cotangent.transpose(0, 2, 1)
    tensors = lax.axis_size("tensor")
    factor = (inputs.shape[2] * tensors) ** (-0.5)
    now, later = spread(inputs, tensors), inputs[1]
    half, velocity, debiased, grad = step(
        0, tensors, push_weight, numerators[0], swapped_all(now), cotangent, momentum[0], factor
    )
    numer, velocity, weight, grads = lax.switch(
        lax.rem(step_index, LEVELS),
        [partial(after_first_half, level, factor) for level in range(LEVELS)],
        half,
        velocity,
        debiased,
        grad,
        later,
        cotangent,
    )
    return numer[None], velocity[None], weight, grads.transpose(0, 2, 1)


def solution(mesh):
    placed = (
        P(None, "tensor", "gossip"),
        P(None, "tensor", "gossip"),
        P("gossip", None, "tensor"),
        P("gossip", None, "tensor"),
        P("gossip"),
        P(),
    )
    return jax.shard_map(
        body,
        mesh=mesh,
        in_specs=placed,
        out_specs=(
            P("gossip", None, "tensor"),
            P("gossip", None, "tensor"),
            P("gossip"),
            P(None, "tensor", "gossip"),
        ),
        check_vma=False,
    )
```

```python
from functools import partial

import jax
import jax.numpy as jnp
from jax import lax
from jax.experimental import pallas as pl
from jax.experimental.pallas import tpu as pltpu
from jax.sharding import PartitionSpec as P

HEAD_DIM = 128
LEVELS = 6
PAD = 16
VMEM_LIMIT = 16 * 1024 * 1024
BF16 = jnp.bfloat16
VMEM = pl.BlockSpec(memory_space=pltpu.VMEM)
SMEM = pl.BlockSpec(memory_space=pltpu.SMEM)
HBM = pl.BlockSpec(memory_space=pltpu.HBM)

CUTS = {
    "plain": lambda k: ((2048, (k,)),),
    "hops": lambda k: ((512, (4,) * (k // 4)),) * 4,
    "both hops": lambda k: ((640, (4,) * 4), (512, (4,) * 4), (512, (4,) * 4), (384, (-12,) * 4)),
    "both": lambda k: ((1664, (k,)), (384, (-24, -24))),
}
LEVEL_PLANS = (
    ("plain", "plain", "late", False, True),
    ("plain", "plain", "late", True, False),
    ("plain", "plain", "late", False, False),
    ("hops", "both", "late", False, False),
    ("both hops", "plain", "late", False, False),
    ("plain", "plain", "joined", False, False),
)


def passed_along(block, distance):
    count = lax.axis_size("gossip")
    route = [(i, (i + distance) % count) for i in range(count)]
    return lax.ppermute(block, "gossip", route)


def swapped_pair(block):
    count = lax.axis_size("tensor")
    return lax.ppermute(block, "tensor", [(i, i ^ 1) for i in range(count)])


def along_x(blocks):
    count = lax.axis_size("tensor")
    groups = [list(range(y, count, 2)) for y in range(2)]
    return lax.all_to_all(blocks, "tensor", 0, 0, axis_index_groups=groups)


def exchange(half, plan):
    parts, at = [], 0
    for number, (size, _) in enumerate(plan):
        size += PAD if number == len(plan) - 1 else 0
        parts.append(half if len(plan) == 1 else half[at : at + size])
        at += size
    for leg in range(max(len(legs) for _, legs in plan)):
        parts = [
            passed_along(part, legs[leg]) if leg < len(legs) else part
            for part, (_, legs) in zip(parts, plan)
        ]
    return parts


def call(kernel, out_shape, operands, name, cost=(0, 1 << 20), in_specs=None, out_specs=None, scratch=()):
    return pl.pallas_call(
        kernel,
        out_shape=out_shape,
        in_specs=in_specs or [VMEM] * len(operands),
        out_specs=out_specs or [VMEM] * len(out_shape),
        scratch_shapes=scratch,
        compiler_params=pltpu.CompilerParams(vmem_limit_bytes=VMEM_LIMIT),
        cost_estimate=pl.CostEstimate(flops=cost[0], bytes_accessed=cost[1], transcendentals=0),
        name=name,
    )(*operands)


def spread_kernel(inputs_ref, now_ref, first, semaphore):
    load = pltpu.make_async_copy(inputs_ref.at[0], first, semaphore)
    load.start()
    load.wait()
    value = first[...]
    for j in range(now_ref.shape[0]):
        now_ref[j, 0] = value


def spread(inputs, count):
    block = inputs.shape[1:]
    return call(
        spread_kernel,
        [jax.ShapeDtypeStruct((count, 1, *block), BF16)],
        [inputs],
        "spread",
        in_specs=[HBM],
        scratch=[pltpu.VMEM(block, BF16), pltpu.SemaphoreType.DMA],
    )[0]


def spread_pair_kernel(mine_ref, other_ref, spread_ref):
    here = lax.rem(lax.axis_index("tensor"), 2) == 0
    mine, other = mine_ref[...], other_ref[...]
    low = jnp.where(here, mine, other)
    high = jnp.where(here, other, mine)
    for x in range(spread_ref.shape[0]):
        spread_ref[x, 0] = low
        spread_ref[x, 1] = high


def spread_pair(mine, other, count):
    return call(
        spread_pair_kernel,
        [jax.ShapeDtypeStruct((count, 2, *mine.shape), BF16)],
        [mine, other],
        "spread_pair",
    )[0]


def head_backward(queries, upstream):
    results = []
    for start in range(0, queries.shape[1], HEAD_DIM):
        q = queries[:, start : start + HEAD_DIM]
        upper = upstream[:, start : start + HEAD_DIM].astype(jnp.float32)
        inverse = lax.rsqrt(jnp.mean(q * q, axis=1, keepdims=True) + 1e-06)
        normed = q * inverse
        inner = jnp.mean(upper * normed, axis=1, keepdims=True)
        results.append(inverse * (upper - normed * inner))
    return jnp.concatenate(results, axis=1)


def repeat(count, unroll, one):
    if unroll >= count:
        for j in range(count):
            one(j)
        return

    def several(turn, carry):
        for k in range(unroll):
            one(turn * unroll + k)
        return carry

    lax.fori_loop(0, count // unroll, several, 0)


def block_rows(j, block):
    return pl.ds(j * block if isinstance(j, int) else pl.multiple_of(j * block, block), block)


def step_kernel(
    factor, unroll, weight_ref, numer, features, upstream, momentum,
    half_out, momentum_out, debiased_out, grad_out, total,
):
    count, block = features.shape[0], features.shape[3]
    weight = jnp.full((1, block), weight_ref[0], jnp.float32)
    scale = 1.0 / weight
    total[...] = jnp.zeros_like(total)

    def query_term(j):
        rows = block_rows(j, block)
        divided = (numer[rows, :].astype(jnp.float32) * scale).astype(BF16)
        debiased_out[rows, :] = divided
        total[...] += jnp.dot(features[j, 0], divided, preferred_element_type=jnp.float32)

    repeat(count, unroll, query_term)
    grad = head_backward(factor * total[...], upstream[...]).astype(BF16)
    grad_out[...] = grad

    def update(j):
        rows = block_rows(j, block)
        grad_weight = factor * lax.dot_general(
            features[j, 0], grad_out[...], (((0,), (0,)), ((), ())), preferred_element_type=jnp.float32
        )
        moved = (0.9 * momentum[rows, :].astype(jnp.float32) + grad_weight).astype(BF16)
        momentum_out[rows, :] = moved
        held = numer[rows, :].astype(jnp.float32)
        half_out[rows, :] = (held - 0.25 * moved.astype(jnp.float32)).astype(BF16)

    repeat(count, unroll, update)
    high = weight.astype(BF16).astype(jnp.float32)
    line = lax.broadcasted_iota(jnp.int32, (PAD, block), 0)
    lines = jnp.where(line == 0, high, jnp.where(line == 1, weight - high, 0.0))
    half_out[pl.ds(count * block, PAD), :] = lines.astype(BF16)


def step(unroll, weight, numer, features, upstream, momentum, factor):
    rows, width = momentum.shape
    tokens = upstream.shape[0]
    operands = [weight, numer, features, upstream, momentum]
    return call(
        partial(step_kernel, factor, unroll),
        [jax.ShapeDtypeStruct((n, width), BF16) for n in (rows + PAD, rows, rows, tokens)],
        operands,
        "optimizer_step",
        (4 * rows * width * tokens, 8 << 20),
        [SMEM] + [VMEM] * 4,
        scratch=[pltpu.VMEM((tokens, width), jnp.float32)],
    )


def average_kernel(sizes, own, *refs):
    came, numer, weight = refs[:-2], refs[-2], refs[-1]
    at, block = 0, 64
    for part, size in zip(came, sizes):

        def one(j, part=part, at=at):
            here = pl.ds(pl.multiple_of(at + j * block, block), block)
            both = own[here, :].astype(jnp.float32)
            both = both + part[pl.ds(pl.multiple_of(j * block, block), block), :].astype(jnp.float32)
            numer[here, :] = (both * 0.5).astype(BF16)

        repeat(size // block, 2, one)
        at += size
    mine = own[pl.ds(at, PAD), :].astype(jnp.float32)
    other = came[-1][pl.ds(sizes[-1], PAD), :].astype(jnp.float32)
    weight[0] = jnp.max((mine[0:1] + mine[1:2] + (other[0:1] + other[1:2])) * 0.5)


def average(own, came, plan, cost):
    rows, width = own.shape[0] - PAD, own.shape[1]
    return call(
        partial(average_kernel, [size for size, _ in plan]),
        [jax.ShapeDtypeStruct((rows, width), BF16), jax.ShapeDtypeStruct((1,), jnp.float32)],
        [own, *came],
        "average",
        (1 << cost, 1 << 20),
        out_specs=[VMEM, SMEM],
    )


def stage_kernel(half_ref, momentum_ref, cotangent_ref, half_out, momentum_out, upstream_out):
    for source, target in ((half_ref, half_out), (momentum_ref, momentum_out)):
        block = 128 if source.shape[0] % 128 == 0 else PAD

        def one(j, source=source, target=target, block=block):
            rows = pl.ds(pl.multiple_of(j * block, block), block)
            target[rows, :] = source[rows, :]

        repeat(source.shape[0] // block, 1, one)
    upstream_out[...] = cotangent_ref[1]


def stage(half, momentum, cotangent):
    shapes = half.shape, momentum.shape, cotangent.shape[1:]
    return call(
        stage_kernel,
        [jax.ShapeDtypeStruct(shape, BF16) for shape in shapes],
        [half, momentum, cotangent],
        "stage",
    )


def blocks_kernel(factor, kept, *refs):
    out = refs[-1]
    count, block = out.shape[0], out.shape[3]
    for slot in range(kept):
        value = refs[slot][1]
        for j in range(count):
            out[j, slot] = value
    pairs = refs[kept:-1]

    def one(j):
        for number in range(len(pairs) // 2):
            debiased, grad = pairs[2 * number], pairs[2 * number + 1]
            part = lax.dot_general(
                grad[...],
                debiased[block_rows(j, block), :],
                (((1,), (1,)), ((), ())),
                preferred_element_type=jnp.float32,
            )
            out[j, kept + number] = (factor * part).astype(BF16)

    if pairs:
        repeat(count, 2, one)


def blocks_for_peers(factor, kept, pairs):
    tokens, width = (kept or pairs[0][1:])[0].shape[-2:]
    count = lax.axis_size("tensor")
    operands = [*kept, *(ref for pair in pairs for ref in pair)]
    return call(
        partial(blocks_kernel, factor, len(kept)),
        [jax.ShapeDtypeStruct((count, len(kept) + len(pairs), tokens, width), BF16)],
        operands,
        "blocks_for_peers",
        (2 * len(pairs) * count * width * width * tokens, 3 << 20),
    )[0]


def total_of(ref, places):
    total = None
    for place in places:
        term = ref[place].astype(jnp.float32)
        total = term if total is None else total + term
    return total


def add_kernel(mine_ref, came_ref, out_ref):
    out_ref[...] = (mine_ref[...] + came_ref[...].astype(jnp.float32)).astype(BF16)


def pair_kernel(in_ref, mine_ref, other_ref):
    count = in_ref.shape[0]
    here = lax.rem(lax.axis_index("tensor"), 2) == 0
    for slot in range(in_ref.shape[2]):
        low, high = (total_of(in_ref, [(x, y, slot) for x in range(count)]) for y in range(2))
        mine_ref[slot] = jnp.where(here, low, high)
        other_ref[slot] = jnp.where(here, high, low).astype(BF16)


def sum_kernel(slot, in_ref, out_ref):
    out_ref[...] = total_of(in_ref, [(j, slot) for j in range(in_ref.shape[0])]).astype(BF16)


def collect_kernel(slots, first_ref, second_ref, out_ref):
    for index, (slot, ref) in enumerate(zip(slots, (first_ref, second_ref))):
        if slot is None:
            out_ref[index] = ref[...]
        else:
            places = [(j, slot) for j in range(ref.shape[0])]
            out_ref[index] = total_of(ref, places).astype(BF16)


def swapped_all(blocks):
    return lax.all_to_all(blocks, "tensor", 0, 0)


def after_first_half(level, factor, half, velocity, debiased, grad, inputs, cotangent):
    first, second, kind, x_gather, x_sum = LEVEL_PLANS[level]
    first = CUTS[first](1 << level)
    second = CUTS[second](1 << ((level + 1) % LEVELS))
    shape, count = inputs.shape[1:], lax.axis_size("tensor")
    one, both = jax.ShapeDtypeStruct(shape, BF16), jax.ShapeDtypeStruct((2, *shape), BF16)
    if x_gather:
        later = inputs[1]
        half, other = lax.optimization_barrier((half, swapped_pair(later)))
        pairs = spread_pair(later, other, count // 2)
        features = along_x(pairs).reshape(count, 1, *shape)
        blocks = pairs
    else:
        terms = [(debiased, grad)] if kind == "joined" else []
        blocks = blocks_for_peers(factor, [inputs], terms)
        features = swapped_all(blocks)
    came = exchange(half, first)
    held, velocity, blocks = lax.optimization_barrier((half, velocity, blocks))
    held, velocity, upstream = stage(held, velocity, cotangent)
    numer, weight = average(held, came, first, 35 if kind == "joined" else 33)
    half, velocity, debiased_2, grad_2 = step(
        4, weight, numer, features, upstream, velocity, factor
    )
    came = exchange(half, second)
    terms = [(debiased_2, grad_2)]
    if kind == "late":
        terms.insert(0, (debiased, grad))
    else:
        grad_in = call(partial(sum_kernel, 1), [one], [features], "sum_terms")[0]
    blocks = blocks_for_peers(factor, [], terms)
    if x_sum:
        swapped = along_x(blocks.reshape(count // 2, 2, *blocks.shape[1:]))
    else:
        swapped = swapped_all(blocks)
    numer, weight = average(half, came, second, 34 if len(second) > 1 else 35)
    swapped, numer = lax.optimization_barrier((swapped, numer))
    if x_sum:
        wide = jax.ShapeDtypeStruct(both.shape, jnp.float32)
        mine, other = call(pair_kernel, [wide, both], [swapped], "sum_pair")
        grads = call(add_kernel, [both], [mine, swapped_pair(other)], "add_pair")[0]
    else:
        slots, parts = ((0, 1), [swapped] * 2) if kind == "late" else ((None, 0), [grad_in, swapped])
        grads = call(partial(collect_kernel, slots), [both], parts, "collect")[0]
    return numer, velocity, weight, grads


def body(inputs, cotangent, numerators, momentum, push_weight, step_index):
    inputs, cotangent = inputs.transpose(0, 2, 1), cotangent.transpose(0, 2, 1)
    tensors = lax.axis_size("tensor")
    factor = (inputs.shape[2] * tensors) ** (-0.5)
    now = spread(inputs, tensors)
    half, velocity, debiased, grad = step(
        tensors, push_weight, numerators[0], swapped_all(now), cotangent[0], momentum[0], factor
    )
    numer, velocity, weight, grads = lax.switch(
        lax.rem(step_index, LEVELS),
        [partial(after_first_half, level, factor) for level in range(LEVELS)],
        half,
        velocity,
        debiased,
        grad,
        inputs,
        cotangent,
    )
    return numer[None], velocity[None], weight, grads.transpose(0, 2, 1)


def solution(mesh):
    placed = (
        P(None, "tensor", "gossip"),
        P(None, "tensor", "gossip"),
        P("gossip", None, "tensor"),
        P("gossip", None, "tensor"),
        P("gossip"),
        P(),
    )
    return jax.shard_map(
        body,
        mesh=mesh,
        in_specs=placed,
        out_specs=(
            P("gossip", None, "tensor"),
            P("gossip", None, "tensor"),
            P("gossip"),
            P(None, "tensor", "gossip"),
        ),
        check_vma=False,
    )
```

```python
from functools import partial

import jax
import jax.numpy as jnp
from jax import lax
from jax.experimental import pallas as pl
from jax.experimental.pallas import tpu as pltpu
from jax.sharding import PartitionSpec as P

HEAD_DIM = 128
LEVELS = 6
PAD = 16
VMEM_LIMIT = 16 * 1024 * 1024
BF16 = jnp.bfloat16
VMEM = pl.BlockSpec(memory_space=pltpu.VMEM)
SMEM = pl.BlockSpec(memory_space=pltpu.SMEM)
HBM = pl.BlockSpec(memory_space=pltpu.HBM)

CUTS = {
    "plain": lambda k: ((2048, (k,)),),
    "hops": lambda k: ((512, (4,) * (k // 4)),) * 4,
    "both hops": lambda k: ((640, (4,) * 4), (512, (4,) * 4), (512, (4,) * 4), (384, (-12,) * 4)),
    "both": lambda k: ((1664, (k,)), (384, (-24, -24))),
}
LEVEL_PLANS = (
    ("plain", "plain", "late", False, True),
    ("plain", "plain", "late", True, False),
    ("plain", "plain", "late", False, False),
    ("hops", "both", "late", False, False),
    ("both hops", "plain", "late", False, False),
    ("plain", "plain", "joined", False, False),
)


def passed_along(block, distance):
    count = lax.axis_size("gossip")
    route = [(i, (i + distance) % count) for i in range(count)]
    return lax.ppermute(block, "gossip", route)


def swapped_pair(block):
    count = lax.axis_size("tensor")
    return lax.ppermute(block, "tensor", [(i, i ^ 1) for i in range(count)])


def along_x(blocks):
    count = lax.axis_size("tensor")
    groups = [list(range(y, count, 2)) for y in range(2)]
    return lax.all_to_all(blocks, "tensor", 0, 0, axis_index_groups=groups)


def exchange(half, plan):
    parts, at = [], 0
    for number, (size, _) in enumerate(plan):
        size += PAD if number == len(plan) - 1 else 0
        parts.append(half if len(plan) == 1 else half[at : at + size])
        at += size
    for leg in range(max(len(legs) for _, legs in plan)):
        parts = [
            passed_along(part, legs[leg]) if leg < len(legs) else part
            for part, (_, legs) in zip(parts, plan)
        ]
    return parts


def call(kernel, out_shape, operands, name, cost=(0, 1 << 20), in_specs=None, out_specs=None, scratch=()):
    return pl.pallas_call(
        kernel,
        out_shape=out_shape,
        in_specs=in_specs or [VMEM] * len(operands),
        out_specs=out_specs or [VMEM] * len(out_shape),
        scratch_shapes=scratch,
        compiler_params=pltpu.CompilerParams(vmem_limit_bytes=VMEM_LIMIT),
        cost_estimate=pl.CostEstimate(flops=cost[0], bytes_accessed=cost[1], transcendentals=0),
        name=name,
    )(*operands)


def spread_kernel(inputs_ref, now_ref, first, semaphore):
    load = pltpu.make_async_copy(inputs_ref.at[0], first, semaphore)
    load.start()
    load.wait()
    value = first[...]
    for j in range(now_ref.shape[0]):
        now_ref[j, 0] = value


def spread(inputs, count):
    block = inputs.shape[1:]
    return call(
        spread_kernel,
        [jax.ShapeDtypeStruct((count, 1, *block), BF16)],
        [inputs],
        "spread",
        in_specs=[HBM],
        scratch=[pltpu.VMEM(block, BF16), pltpu.SemaphoreType.DMA],
    )[0]


def spread_pair_kernel(mine_ref, other_ref, spread_ref):
    here = lax.rem(lax.axis_index("tensor"), 2) == 0
    mine, other = mine_ref[...], other_ref[...]
    low = jnp.where(here, mine, other)
    high = jnp.where(here, other, mine)
    for x in range(spread_ref.shape[0]):
        spread_ref[x, 0] = low
        spread_ref[x, 1] = high


def spread_pair(mine, other, count):
    return call(
        spread_pair_kernel,
        [jax.ShapeDtypeStruct((count, 2, *mine.shape), BF16)],
        [mine, other],
        "spread_pair",
    )[0]


def head_backward(queries, upstream):
    results = []
    for start in range(0, queries.shape[1], HEAD_DIM):
        q = queries[:, start : start + HEAD_DIM]
        upper = upstream[:, start : start + HEAD_DIM].astype(jnp.float32)
        inverse = lax.rsqrt(jnp.mean(q * q, axis=1, keepdims=True) + 1e-06)
        normed = q * inverse
        inner = jnp.mean(upper * normed, axis=1, keepdims=True)
        results.append(inverse * (upper - normed * inner))
    return jnp.concatenate(results, axis=1)


def repeat(count, unroll, one):
    if unroll >= count:
        for j in range(count):
            one(j)
        return

    def several(turn, carry):
        for k in range(unroll):
            one(turn * unroll + k)
        return carry

    lax.fori_loop(0, count // unroll, several, 0)


def block_rows(j, block):
    return pl.ds(j * block if isinstance(j, int) else pl.multiple_of(j * block, block), block)


def step_kernel(
    factor, unroll, averaged, weight_ref, numer, *refs
):
    came, refs = (refs[0], refs[1:]) if averaged else (None, refs)
    features, upstream, momentum, half_out, momentum_out, debiased_out, grad_out, total = refs[:8]
    own, numer = (numer, refs[8]) if averaged else (None, numer)
    count, block = features.shape[0], features.shape[3]
    weight = jnp.full((1, block), weight_ref[0], jnp.float32)
    scale = 1.0 / weight
    total[...] = jnp.zeros_like(total)

    def query_term(j):
        rows = block_rows(j, block)
        if averaged:
            both = own[rows, :].astype(jnp.float32) + came[rows, :].astype(jnp.float32)
            numer[rows, :] = (both * 0.5).astype(BF16)
        divided = (numer[rows, :].astype(jnp.float32) * scale).astype(BF16)
        debiased_out[rows, :] = divided
        total[...] += jnp.dot(features[j, 0], divided, preferred_element_type=jnp.float32)

    repeat(count, unroll, query_term)
    grad = head_backward(factor * total[...], upstream[...]).astype(BF16)
    grad_out[...] = grad

    def update(j):
        rows = block_rows(j, block)
        grad_weight = factor * lax.dot_general(
            features[j, 0], grad_out[...], (((0,), (0,)), ((), ())), preferred_element_type=jnp.float32
        )
        moved = (0.9 * momentum[rows, :].astype(jnp.float32) + grad_weight).astype(BF16)
        momentum_out[rows, :] = moved
        held = numer[rows, :].astype(jnp.float32)
        half_out[rows, :] = (held - 0.25 * moved.astype(jnp.float32)).astype(BF16)

    repeat(count, unroll, update)
    high = weight.astype(BF16).astype(jnp.float32)
    line = lax.broadcasted_iota(jnp.int32, (PAD, block), 0)
    lines = jnp.where(line == 0, high, jnp.where(line == 1, weight - high, 0.0))
    half_out[pl.ds(count * block, PAD), :] = lines.astype(BF16)


def step(unroll, weight, state, features, upstream, momentum, factor):
    rows, width = momentum.shape
    tokens = upstream.shape[0]
    averaged = len(state) > 1
    operands = [weight, *state, features, upstream, momentum]
    return call(
        partial(step_kernel, factor, unroll, averaged),
        [jax.ShapeDtypeStruct((n, width), BF16) for n in (rows + PAD, rows, rows, tokens)],
        operands,
        "optimizer_step",
        (4 * rows * width * tokens, 8 << 20),
        [SMEM] + [VMEM] * (len(operands) - 1),
        scratch=[pltpu.VMEM((tokens, width), jnp.float32)] + [pltpu.VMEM((rows, width), BF16)] * averaged,
    )


def average_kernel(sizes, own, *refs):
    came, numer, weight = refs[:-2], refs[-2], refs[-1]
    at, block = 0, 64
    for part, size in zip(came, sizes):

        def one(j, part=part, at=at):
            here = pl.ds(pl.multiple_of(at + j * block, block), block)
            both = own[here, :].astype(jnp.float32)
            both = both + part[pl.ds(pl.multiple_of(j * block, block), block), :].astype(jnp.float32)
            numer[here, :] = (both * 0.5).astype(BF16)

        repeat(size // block, 2, one)
        at += size
    mine = own[pl.ds(at, PAD), :].astype(jnp.float32)
    other = came[-1][pl.ds(sizes[-1], PAD), :].astype(jnp.float32)
    weight[0] = jnp.max((mine[0:1] + mine[1:2] + (other[0:1] + other[1:2])) * 0.5)


def weight_kernel(own, came, weight, mine, other, semaphores):
    tail = pl.ds(own.shape[0] - PAD, PAD)
    copies = [
        pltpu.make_async_copy(source.at[tail, :], target, semaphores.at[k])
        for k, (source, target) in enumerate(((own, mine), (came, other)))
    ]
    for copy in copies:
        copy.start()
    for copy in copies:
        copy.wait()
    left, right = mine[...].astype(jnp.float32), other[...].astype(jnp.float32)
    weight[0] = jnp.max((left[0:1] + left[1:2] + (right[0:1] + right[1:2])) * 0.5)


def average_weight(own, came, cost):
    rest = pltpu.VMEM((PAD, own.shape[1]), BF16)
    return call(
        weight_kernel,
        [jax.ShapeDtypeStruct((1,), jnp.float32)],
        [own, came],
        "average_weight",
        (1 << cost, 1 << 20),
        in_specs=[pl.BlockSpec(memory_space=pl.ANY)] * 2,
        out_specs=[SMEM],
        scratch=[rest, rest, pltpu.SemaphoreType.DMA((2,))],
    )[0]


def average(own, came, plan, cost):
    rows, width = own.shape[0] - PAD, own.shape[1]
    return call(
        partial(average_kernel, [size for size, _ in plan]),
        [jax.ShapeDtypeStruct((rows, width), BF16), jax.ShapeDtypeStruct((1,), jnp.float32)],
        [own, *came],
        "average",
        (1 << cost, 1 << 20),
        out_specs=[VMEM, SMEM],
    )


def stage_kernel(half_ref, momentum_ref, cotangent_ref, half_out, momentum_out, upstream_out):
    for source, target in ((half_ref, half_out), (momentum_ref, momentum_out)):
        block = 128 if source.shape[0] % 128 == 0 else PAD

        def one(j, source=source, target=target, block=block):
            rows = pl.ds(pl.multiple_of(j * block, block), block)
            target[rows, :] = source[rows, :]

        repeat(source.shape[0] // block, 1, one)
    upstream_out[...] = cotangent_ref[1]


def stage(half, momentum, cotangent):
    shapes = half.shape, momentum.shape, cotangent.shape[1:]
    return call(
        stage_kernel,
        [jax.ShapeDtypeStruct(shape, BF16) for shape in shapes],
        [half, momentum, cotangent],
        "stage",
    )


def blocks_kernel(factor, kept, *refs):
    out = refs[-1]
    count, block = out.shape[0], out.shape[3]
    for slot in range(kept):
        value = refs[slot][1]
        for j in range(count):
            out[j, slot] = value
    pairs = refs[kept:-1]

    def one(j):
        for number in range(len(pairs) // 2):
            debiased, grad = pairs[2 * number], pairs[2 * number + 1]
            part = lax.dot_general(
                grad[...],
                debiased[block_rows(j, block), :],
                (((1,), (1,)), ((), ())),
                preferred_element_type=jnp.float32,
            )
            out[j, kept + number] = (factor * part).astype(BF16)

    if pairs:
        repeat(count, 2, one)


def blocks_for_peers(factor, kept, pairs):
    tokens, width = (kept or pairs[0][1:])[0].shape[-2:]
    count = lax.axis_size("tensor")
    operands = [*kept, *(ref for pair in pairs for ref in pair)]
    return call(
        partial(blocks_kernel, factor, len(kept)),
        [jax.ShapeDtypeStruct((count, len(kept) + len(pairs), tokens, width), BF16)],
        operands,
        "blocks_for_peers",
        (2 * len(pairs) * count * width * width * tokens, 3 << 20),
    )[0]


def total_of(ref, places):
    total = None
    for place in places:
        term = ref[place].astype(jnp.float32)
        total = term if total is None else total + term
    return total


def add_kernel(mine_ref, came_ref, out_ref):
    out_ref[...] = (mine_ref[...] + came_ref[...].astype(jnp.float32)).astype(BF16)


def pair_kernel(in_ref, mine_ref, other_ref):
    count = in_ref.shape[0]
    here = lax.rem(lax.axis_index("tensor"), 2) == 0
    for slot in range(in_ref.shape[2]):
        low, high = (total_of(in_ref, [(x, y, slot) for x in range(count)]) for y in range(2))
        mine_ref[slot] = jnp.where(here, low, high)
        other_ref[slot] = jnp.where(here, high, low).astype(BF16)


def sum_kernel(slot, in_ref, out_ref):
    out_ref[...] = total_of(in_ref, [(j, slot) for j in range(in_ref.shape[0])]).astype(BF16)


def collect_kernel(slots, first_ref, second_ref, out_ref):
    for index, (slot, ref) in enumerate(zip(slots, (first_ref, second_ref))):
        if slot is None:
            out_ref[index] = ref[...]
        else:
            places = [(j, slot) for j in range(ref.shape[0])]
            out_ref[index] = total_of(ref, places).astype(BF16)


def swapped_all(blocks):
    return lax.all_to_all(blocks, "tensor", 0, 0)


def after_first_half(level, factor, half, velocity, debiased, grad, inputs, cotangent):
    first, second, kind, x_gather, x_sum = LEVEL_PLANS[level]
    first = CUTS[first](1 << level)
    second = CUTS[second](1 << ((level + 1) % LEVELS))
    shape, count = inputs.shape[1:], lax.axis_size("tensor")
    one, both = jax.ShapeDtypeStruct(shape, BF16), jax.ShapeDtypeStruct((2, *shape), BF16)
    if x_gather:
        later = inputs[1]
        half, other = lax.optimization_barrier((half, swapped_pair(later)))
        pairs = spread_pair(later, other, count // 2)
        features = along_x(pairs).reshape(count, 1, *shape)
        blocks = pairs
    else:
        terms = [(debiased, grad)] if kind == "joined" else []
        blocks = blocks_for_peers(factor, [inputs], terms)
        features = swapped_all(blocks)
    came = exchange(half, first)
    cost = 35 if kind == "joined" else 33
    if len(first) > 1:
        held, velocity, blocks = lax.optimization_barrier((half, velocity, blocks))
        held, velocity, upstream = stage(held, velocity, cotangent)
        numer, weight = average(held, came, first, cost)
        state = [numer]
    else:
        weight, upstream = average_weight(half, came[0], cost), cotangent[1]
        state = [half, came[0]]
    half, velocity, debiased_2, grad_2 = step(
        4, weight, state, features, upstream, velocity, factor
    )
    came = exchange(half, second)
    terms = [(debiased_2, grad_2)]
    if kind == "late":
        terms.insert(0, (debiased, grad))
    else:
        grad_in = call(partial(sum_kernel, 1), [one], [features], "sum_terms")[0]
    blocks = blocks_for_peers(factor, [], terms)
    if x_sum:
        swapped = along_x(blocks.reshape(count // 2, 2, *blocks.shape[1:]))
    else:
        swapped = swapped_all(blocks)
    numer, weight = average(half, came, second, 34 if len(second) > 1 else 35)
    swapped, numer = lax.optimization_barrier((swapped, numer))
    if x_sum:
        wide = jax.ShapeDtypeStruct(both.shape, jnp.float32)
        mine, other = call(pair_kernel, [wide, both], [swapped], "sum_pair")
        grads = call(add_kernel, [both], [mine, swapped_pair(other)], "add_pair")[0]
    else:
        slots, parts = ((0, 1), [swapped] * 2) if kind == "late" else ((None, 0), [grad_in, swapped])
        grads = call(partial(collect_kernel, slots), [both], parts, "collect")[0]
    return numer, velocity, weight, grads


def body(inputs, cotangent, numerators, momentum, push_weight, step_index):
    inputs, cotangent = inputs.transpose(0, 2, 1), cotangent.transpose(0, 2, 1)
    tensors = lax.axis_size("tensor")
    factor = (inputs.shape[2] * tensors) ** (-0.5)
    now = spread(inputs, tensors)
    half, velocity, debiased, grad = step(
        tensors, push_weight, [numerators[0]], swapped_all(now), cotangent[0], momentum[0], factor
    )
    numer, velocity, weight, grads = lax.switch(
        lax.rem(step_index, LEVELS),
        [partial(after_first_half, level, factor) for level in range(LEVELS)],
        half,
        velocity,
        debiased,
        grad,
        inputs,
        cotangent,
    )
    return numer[None], velocity[None], weight, grads.transpose(0, 2, 1)


def solution(mesh):
    placed = (
        P(None, "tensor", "gossip"),
        P(None, "tensor", "gossip"),
        P("gossip", None, "tensor"),
        P("gossip", None, "tensor"),
        P("gossip"),
        P(),
    )
    return jax.shard_map(
        body,
        mesh=mesh,
        in_specs=placed,
        out_specs=(
            P("gossip", None, "tensor"),
            P("gossip", None, "tensor"),
            P("gossip"),
            P(None, "tensor", "gossip"),
        ),
        check_vma=False,
    )
```
